32 devices in a mesh: dp: 4 (over z), expert: 8 (over y, x, core).
Axes of the slice: x: 2, y: 2, z: 4, core: 2. Of those that a mesh axis runs over, the one named last changes fastest.
Arguments:
- tokens: bfloat16 [4096, 2880], P(('expert', 'dp')), may hold values from -6 to 6
- passes_through: int32 [4096], P(('expert', 'dp')), may hold values from 0 to 1, as said below
- keep_weight: float32 [4096], P(('expert', 'dp')), may hold values from 0.25 to 2
- norm_gain: float32 [2880], replicated, may hold values from 0.5 to 1.5
- routes: int32 [8, 32, 4], P('expert'), may hold values from 0 to 7, all different within a row; in each aligned block of 32 rows (0 to 31, 32 to 63, ..., all dimensions but the last counted through in order) at most 20 rows name the same one
- gate_values: float32 [8, 32, 4], P('expert'), may hold values from 0.05 to 1
- w_gate: bfloat16 [8, 2880, 2880], P('expert', None, 'dp'), may hold values from -0.109375 to 0.109375
- w_up: bfloat16 [8, 2880, 2880], P('expert', None, 'dp'), may hold values from -0.109375 to 0.109375
- w_down: bfloat16 [8, 2880, 2880], P('expert', 'dp'), may hold values from -0.109375 to 0.109375
Outputs:
- mixed: bfloat16 [4096, 2880], P(('expert', 'dp'))
The draws below stay inside these ranges and needn't reach their ends.
Inputs may be any that keep to these rules, and one draw needn't show every extreme that they name: `passes_through`: each sequence of 512 tokens has exactly 32 survivors. The 128 tokens of one index of dp hold at most 24 survivors, and in every sequence one such group holds exactly 24. `routes`: the 4 ids of a survivor differ. Within one sequence no expert is named more than 20 times, a bound that some block reaches.
All inputs are finite; a program needn't handle non-finite values.
Results may differ from the reference program's by a relative error of at most 0.005.
Values may be sent and summed in bfloat16 or wider, within the bound.
A program may use at most 64 MiB of HBM per device.

```python
import math
import jax
import jax.numpy as jnp
import numpy as np
from jax import lax

MODEL_WIDTH = 2880
FF = 2880
TOPK = 4
TOK_DEV = 128
EXPERTS = 8
MAXLOC = 24
SEQUENCE_LENGTH = 512
SEQUENCE_COUNT = 8
SEQ_KEEP = 32
CAP_COL = 20
TOKENS = 4096
N_DP = 4


def draw_passes_through(key, part):
    key = jax.random.fold_in(key, 11)
    pieces = SEQUENCE_LENGTH // TOK_DEV

    def one_sequence(seq_key):
        initial_random_seed, second_key, third_key = jax.random.split(seq_key, 3)
        hottest = jax.random.randint(initial_random_seed, (), 0, pieces)
        spare = (pieces - 1) * MAXLOC
        chosen = jax.random.permutation(second_key, spare) < SEQ_KEEP - MAXLOC
        others = jnp.sum(chosen.reshape(pieces - 1, MAXLOC).astype(jnp.int32), axis=1)
        index_all = jnp.arange(pieces, dtype=jnp.int32)
        other_index = jnp.clip(index_all - (index_all > hottest).astype(jnp.int32), 0, pieces - 2)
        counts_all = jnp.where(index_all == hottest, MAXLOC, others[other_index])
        piece_keys = jax.random.split(third_key, pieces)
        ranking = jax.vmap(lambda sub_key: jax.random.permutation(sub_key, TOK_DEV))(piece_keys)
        return (ranking < counts_all[:, None]).astype(jnp.int32).reshape(SEQUENCE_LENGTH)
    seq_keys = jax.random.split(key, SEQUENCE_COUNT)
    return jax.vmap(one_sequence)(seq_keys).reshape(SEQUENCE_COUNT * SEQUENCE_LENGTH)


def shard_levels(own_key, shape, cuts, least, largest):
    factor_of = 1.0
    for axis_at, blocks in cuts:
        steps = jax.random.uniform(jax.random.fold_in(jax.random.fold_in(own_key, 6), axis_at), (blocks,), jnp.float32, least / len(cuts), largest / len(cuts))
        factor_of = factor_of * jnp.repeat(jnp.exp(steps), shape[axis_at] // blocks).reshape((-1,) + (1,) * (len(shape) - 1 - axis_at))
    return factor_of


def routed_block(stream_key, own, number, rows, count, top, most, slope):
    sequence = jax.random.permutation(stream_key, count)
    packed, common = shares(count, rows * top, most, slope, True), shares(count, rows * top, most, slope, False)
    places = jnp.arange(count)

    def named(tallies, rotation):
        used = int((tallies > 0).sum())
        fixed = max(1, used // 4)
        moved = fixed + (places - fixed + rotation * (used - fixed)) % max(1, count - fixed)
        return jnp.zeros((count,), jnp.int32).at[sequence[jnp.where(places < fixed, places, moved)]].set(jnp.asarray(tallies, jnp.int32))

    tallies = jnp.where(number % 4 == 0, named(packed, number // 4), named(common, number - number // 4 - 1))
    mixed = jax.random.permutation(jax.random.fold_in(own, 3), count)
    giver, sink = mixed[0:count // 2 * 2:2], mixed[1:count // 2 * 2:2]
    slack = jnp.minimum(tallies[giver] - 1, most - tallies[sink]) // 2
    slack = jnp.where((giver == sequence[0]) | (sink == sequence[0]) | (tallies[sink] == 0), 0, jnp.maximum(slack, 0))
    moved = jax.random.randint(jax.random.fold_in(own, 4), (count // 2,), 0, 1 << 20) % (slack + 1)
    tallies = tallies.at[giver].add(-moved).at[sink].add(moved)
    labels = jnp.searchsorted(jnp.cumsum(tallies), jnp.arange(rows * top), side="right").astype(jnp.int32)
    table = labels.reshape(top, rows).T
    table = table[jax.random.permutation(jax.random.fold_in(own, 1), rows)]
    rotation = jax.random.randint(jax.random.fold_in(own, 2), (rows, 1), 0, top)
    return jnp.take_along_axis(table, (jnp.arange(top)[None, :] + rotation) % top, axis=1)


def shares(amount, total, limit, lean, full):
    portions = [(1 << 20) // math.isqrt(standing ** lean) + 1 for standing in range(1, amount + 1)]
    largest = limit if full else min(limit, max(-(-total // amount), total * portions[0] // sum(portions)))
    least = 1 if total - largest >= amount - 1 else 0
    holding, rest = [largest] + [least] * (amount - 1), total - largest - least * (amount - 1)
    while rest > 0:
        free = [i for i in range(1, amount) if holding[i] < largest] or [i for i in range(1, amount) if holding[i] < limit]
        mass, left = sum([portions[i] for i in free]), rest
        for i in free:
            addition = min(limit - holding[i], max(1, left * portions[i] // mass), rest)
            holding[i] = holding[i] + addition
            rest = rest - addition
    return np.array(holding)


def gaussian(key, dims, width, reach, cuts=(), held_as=jnp.bfloat16):
    entries = jax.random.normal(key, dims, jnp.float32) * width
    if len(cuts) > 0:
        entries = shard_levels(key, dims, cuts, -0.22, 0.18) * entries
    return jnp.clip(entries, min=-reach, max=reach).astype(held_as)


def setup_inputs(seed: int = 0) -> dict:
    arg_keys = jax.random.split(jax.random.key(seed), 10)
    tokens = gaussian(arg_keys[0], (TOKENS, MODEL_WIDTH), 1.0, 6.0, ((0, 32),))
    passes_through = draw_passes_through(jax.random.fold_in(arg_keys[9], 71), 0)
    keep_weight = jnp.clip(jnp.exp(math.log(2.0) - 2.0794415 * jax.random.uniform(arg_keys[2], (TOKENS,), jnp.float32) ** shard_levels(arg_keys[2], (TOKENS,), ((0, 32),), -0.2, 0.2)), 0.25, 2.0)
    norm_gain = jnp.clip(1.0 + 0.1 * jax.random.normal(arg_keys[3], (MODEL_WIDTH,), jnp.float32), 0.5, 1.5)
    routes_keys = jax.random.split(jax.random.fold_in(arg_keys[4], 1), SEQUENCE_COUNT * SEQ_KEEP // SEQ_KEEP)
    routes_turns = jax.random.permutation(jax.random.fold_in(arg_keys[4], 3), SEQUENCE_COUNT * SEQ_KEEP // SEQ_KEEP)
    routes = jax.vmap(lambda own, number: routed_block(jax.random.fold_in(arg_keys[4], 2), own, number, SEQ_KEEP, EXPERTS, TOPK, CAP_COL, 1))(routes_keys, routes_turns).reshape((SEQUENCE_COUNT, SEQ_KEEP, TOPK))
    gate_values = jnp.clip(jnp.exp(math.log(1.0) - 2.9957323 * jax.random.uniform(arg_keys[5], (SEQUENCE_COUNT, SEQ_KEEP, TOPK), jnp.float32) ** shard_levels(arg_keys[5], (SEQUENCE_COUNT, SEQ_KEEP, TOPK), ((0, 8),), -0.2, 0.2)), 0.05, 1.0)
    w_gate = gaussian(arg_keys[6], (EXPERTS, MODEL_WIDTH, FF), MODEL_WIDTH ** -0.5, 0.109375, ((0, 8), (2, 4)))
    w_up = gaussian(arg_keys[7], (EXPERTS, MODEL_WIDTH, FF), MODEL_WIDTH ** -0.5, 0.109375, ((0, 8), (2, 4)))
    w_down = gaussian(arg_keys[8], (EXPERTS, FF, MODEL_WIDTH), FF ** -0.5, 0.109375, ((0, 8), (1, 4)))
    return dict(tokens=tokens, passes_through=passes_through, keep_weight=keep_weight, norm_gain=norm_gain, routes=routes, gate_values=gate_values, w_gate=w_gate, w_up=w_up, w_down=w_down)


norm_eps = 1e-05

def reference(tokens, passes_through, keep_weight, norm_gain, routes, gate_values, w_gate, w_up, w_down):
    values = tokens.astype(jnp.float32)
    scaling = lax.rsqrt(lax.optimization_barrier(jnp.mean(values * values, axis=-1, keepdims=True)) + norm_eps)
    normalized_rows = (values * scaling * norm_gain).astype(jnp.bfloat16)
    active_flags = passes_through.reshape(SEQUENCE_COUNT, SEQUENCE_LENGTH)
    token_positions = jnp.argsort(1 - active_flags, axis=1, stable=True)[:, :SEQ_KEEP].astype(jnp.int32)
    kept_tokens = jnp.take_along_axis(normalized_rows.reshape(SEQUENCE_COUNT, SEQUENCE_LENGTH, MODEL_WIDTH), token_positions[:, :, None], axis=1)
    flat_routes = routes.reshape(SEQUENCE_COUNT, SEQ_KEEP * TOPK)
    onehot = (flat_routes[:, :, None] == jnp.arange(EXPERTS, dtype=jnp.int32)[None, None, :]).astype(jnp.int32)
    slot_rank = lax.optimization_barrier(jnp.sum((jnp.cumsum(onehot, axis=1) - onehot) * onehot, axis=2)).astype(jnp.int32)
    sequence_index = jnp.broadcast_to(jnp.arange(SEQUENCE_COUNT, dtype=jnp.int32)[:, None], flat_routes.shape)
    gathered_row = jnp.broadcast_to(jnp.repeat(jnp.arange(SEQ_KEEP, dtype=jnp.int32), TOPK)[None, :], flat_routes.shape)
    assigned_expert = kept_tokens[sequence_index, gathered_row]
    storage_arrays = jnp.zeros((EXPERTS, SEQUENCE_COUNT, CAP_COL, MODEL_WIDTH), jnp.bfloat16).at[flat_routes, sequence_index, slot_rank].set(assigned_expert)
    hidden_block = FF // N_DP

    def expert_rows(operands):
        block, gate_matrix, up_matrix, down_matrix = operands
        rows_all = block.reshape(SEQUENCE_COUNT * CAP_COL, MODEL_WIDTH)
        gate_proj = jnp.dot(rows_all, gate_matrix, preferred_element_type=jnp.float32)
        up_proj = jnp.dot(rows_all, up_matrix, preferred_element_type=jnp.float32)
        hidden = ((up_proj + 1.0) * gate_proj * jax.nn.sigmoid(1.702 * gate_proj)).astype(jnp.bfloat16)
        split_hidden = hidden.astype(jnp.float32).reshape(SEQUENCE_COUNT * CAP_COL, N_DP, hidden_block)
        split_down = down_matrix.astype(jnp.float32).reshape(N_DP, hidden_block, MODEL_WIDTH)
        partials = jnp.einsum('rnf,nfd->nrd', split_hidden, split_down)
        rounded = lax.optimization_barrier(partials.astype(jnp.bfloat16))
        summed = lax.optimization_barrier(jnp.sum(rounded.astype(jnp.float32), axis=0))
        return summed.astype(jnp.bfloat16).reshape(SEQUENCE_COUNT, CAP_COL, MODEL_WIDTH)
    outputs = lax.map(expert_rows, (storage_arrays, w_gate, w_up, w_down))
    picked = outputs[flat_routes, sequence_index, slot_rank].astype(jnp.float32).reshape(SEQUENCE_COUNT, SEQ_KEEP, TOPK, MODEL_WIDTH)
    mixture = lax.optimization_barrier(jnp.sum(gate_values[:, :, :, None] * picked, axis=2)).astype(jnp.bfloat16)
    own_values = values.reshape(SEQUENCE_COUNT, SEQUENCE_LENGTH, MODEL_WIDTH)
    keep_seq = keep_weight.reshape(SEQUENCE_COUNT, SEQUENCE_LENGTH)
    rows_index = jnp.broadcast_to(jnp.arange(SEQUENCE_COUNT, dtype=jnp.int32)[:, None], token_positions.shape)
    updated = own_values[rows_index, token_positions] + keep_seq[rows_index, token_positions][:, :, None] * mixture.astype(jnp.float32)
    result = own_values.at[rows_index, token_positions].set(updated)
    return result.reshape(TOKENS, MODEL_WIDTH).astype(jnp.bfloat16)
```

```python
import jax
import jax.numpy as jnp
from jax import lax
from jax.experimental import pallas as pl
from jax.experimental.pallas import tpu as pltpu
from jax.sharding import PartitionSpec as P

CHUNK = 768
LANES = 128
HALF = 16


def chunks_of(width):
    starts = list(range(0, width, CHUNK))
    return [(s, min(CHUNK, width - s)) for s in starts]


def fused_kernel(
    tokens_hbm, passes_ref, keep_ref, gain_ref, routes_ref, gates_ref, wg_hbm, wu_hbm, wd_hbm,
    out_ref,
    tokens, wg, wu, wd, cnt, gb, own, zin, zsend, tot, x, acc_g, acc_u, hid, ob, rb, sb, rr,
    ret, zin2, zsend2,
    ld_sem, cnt_s, cnt_r, gb_s, gb_r, z_s, z_r, a_s, a_r, b_s, b_r, d_s, d_r, e_s, e_r, z2_s, z2_r,
):
    z, me = lax.axis_index("dp"), lax.axis_index("expert")
    n_z, n_e = lax.axis_size("dp"), lax.axis_size("expert")
    width = tokens.shape[1]
    chunks = chunks_of(width)
    n_c = len(chunks)
    span = [pl.ds(0, -(-w // LANES) * LANES) for _, w in chunks]
    core = lax.rem(me, 2)
    sibling = me + 1 - 2 * core
    low = z < 2
    edge = jnp.logical_or(z == 0, z == n_z - 1)
    middle = jnp.logical_not(edge)
    inward = jnp.where(low, z + 1, z - 1)
    outward = jnp.where(z == 1, 0, n_z - 1)
    lands = jnp.where(edge, 0, 1)
    f32, bf16 = jnp.float32, jnp.bfloat16

    loads = [
        pltpu.make_async_copy(tokens_hbm, tokens, ld_sem.at[0]),
        pltpu.make_async_copy(wg_hbm, wg, ld_sem.at[1]),
        pltpu.make_async_copy(wu_hbm, wu, ld_sem.at[2]),
        pltpu.make_async_copy(wd_hbm, wd, ld_sem.at[3]),
    ]
    for load in loads:
        load.start()

    barrier = pltpu.get_barrier_semaphore()
    for r in range(1, n_z):
        pl.semaphore_signal(barrier, inc=1, device_id={"dp": lax.rem(z + r, n_z)})
    for r in range(1, n_e):
        pl.semaphore_signal(barrier, inc=1, device_id={"expert": lax.rem(me + r, n_e)})

    flags = passes_ref[...].astype(f32)
    t_tok = flags.shape[1]
    sub = lax.broadcasted_iota(jnp.int32, (t_tok, t_tok), 0)
    lane = lax.broadcasted_iota(jnp.int32, (t_tok, t_tok), 1)
    wide = jnp.broadcast_to(flags, (t_tok, t_tok))
    rank_col = jnp.sum(jnp.where(lane <= sub, wide, 0.0), axis=1, keepdims=True) - 1.0
    flag_col = jnp.sum(jnp.where(lane == sub, wide, 0.0), axis=1, keepdims=True)
    keep_col = jnp.sum(
        jnp.where(lane == sub, jnp.broadcast_to(keep_ref[...], (t_tok, t_tok)), 0.0),
        axis=1, keepdims=True,
    )
    rank_row = jnp.sum(jnp.where(sub <= lane, flag_col, 0.0), axis=0, keepdims=True) - 1.0

    cnt[z] = jnp.broadcast_to(flags, cnt.shape[1:])
    seq_keep, top = routes_ref.shape
    e_lane = lax.broadcasted_iota(jnp.int32, (seq_keep, LANES), 1)
    weights = jnp.zeros((seq_keep, LANES), f32)
    for k in range(top):
        weights += jnp.where(routes_ref[:, k:k + 1] == e_lane, gates_ref[:, k:k + 1], 0.0)
    gb[:, me] = weights.reshape(2, HALF, LANES)

    pl.semaphore_wait(barrier, n_z - 1 + n_e - 1)
    sends = []

    def send(src, dst, ssem, rsem, device):
        copy = pltpu.make_async_remote_copy(
            src_ref=src, dst_ref=dst, send_sem=ssem, recv_sem=rsem, device_id=device,
            device_id_type=pl.DeviceIdType.MESH,
        )
        copy.start()
        return copy

    def arrived(ref, sem):
        pltpu.make_async_copy(ref, ref, sem).wait()

    for r in range(1, n_z):
        sends.append(send(cnt.at[z], cnt.at[z], cnt_s.at[r - 1], cnt_r, {"dp": lax.rem(z + r, n_z)}))
    for r in range(1, n_e):
        sends.append(
            send(gb.at[:, me], gb.at[:, me], gb_s.at[r - 1], gb_r, {"expert": lax.rem(me + r, n_e)})
        )

    loads[0].wait()
    arrived(cnt.at[pl.ds(0, n_z - 1)], cnt_r)
    offset = jnp.zeros((1, 1), f32)
    for other in range(n_z):
        total = jnp.sum(cnt[other, 0:1, :], axis=1, keepdims=True)
        offset += jnp.where(other < z, total, 0.0)
    s_sub = lax.broadcasted_iota(jnp.int32, (seq_keep, t_tok), 0).astype(f32)
    picker = jnp.where((rank_row + offset == s_sub) & (flags > 0.5), 1.0, 0.0).astype(bf16)
    s_lane = lax.broadcasted_iota(jnp.int32, (t_tok, seq_keep), 1).astype(f32)
    spread_pick = jnp.where((rank_col + offset == s_lane) & (flag_col > 0.5), 1.0, 0.0).astype(bf16)

    compact = jnp.dot(picker, tokens[...], preferred_element_type=f32)
    scaling = lax.rsqrt(jnp.sum(compact * compact, axis=1, keepdims=True) * (1.0 / width) + 1e-05)
    normed = (compact * scaling * gain_ref[...]).astype(bf16)

    @pl.when(edge)
    def _():
        zin[0] = jnp.zeros_like(zin[0])
        zin2[0] = jnp.zeros_like(zin2[0])

    for k, (start, w) in enumerate(chunks):
        own[k, :, 0:w] = normed[:, start:start + w]

    def line_copy(src, dst, k, which, s_sems, r_sems, device):
        return pltpu.make_async_remote_copy(
            src_ref=src, dst_ref=dst, send_sem=s_sems.at[which, k], recv_sem=r_sems,
            device_id={"dp": device}, device_id_type=pl.DeviceIdType.MESH,
        )

    def near(k, mine, into, out, s_sems, r_sems):
        @pl.when(middle)
        def _():
            arrived(into.at[0, k, :, span[k]], r_sems.at[0, k])

        out[0, k] = (mine[k].astype(f32) + into[0, k].astype(f32)).astype(bf16)
        line_copy(
            out.at[0, k, :, span[k]], into.at[lands, k, :, span[k]], k, 0, s_sems,
            r_sems.at[lands, k], inward,
        ).start()

    def far(k, mine, into, out, s_sems, r_sems):
        arrived(into.at[1, k, :, span[k]], r_sems.at[1, k])
        part = mine[k].astype(f32) + into[1, k].astype(f32)

        @pl.when(middle)
        def _():
            out[1, k] = part.astype(bf16)
            line_copy(
                out.at[1, k, :, span[k]], into.at[1, k, :, span[k]], k, 1, s_sems,
                r_sems.at[1, k], outward,
            ).start()

        return (part + into[0, k].astype(f32)).astype(bf16)

    def line_drain(k, out, s_sems):
        arrived(out.at[0, k, :, span[k]], s_sems.at[0, k])

        @pl.when(middle)
        def _():
            arrived(out.at[1, k, :, span[k]], s_sems.at[1, k])

    line_in = (own, zin, zsend, z_s, z_r)
    line_out = (ret, zin2, zsend2, z2_s, z2_r)

    def s_near(k):
        near(k, *line_in)

    def s_far(k):
        tot[k] = far(k, *line_in).reshape(2, HALF, CHUNK)
        x[k, core, me] = tot[k, core]
        for r in range(1, n_e):
            to = lax.rem(me + r, n_e)
            side = lax.rem(to, 2)
            sends.append(send(
                tot.at[k, side, :, span[k]], x.at[k, side, me, :, span[k]],
                a_s.at[k, r - 1], a_r.at[k], {"expert": to},
            ))

    def s_swap(k):
        arrived(x.at[k, core, pl.ds(0, n_e - 1), :, span[k]], a_r.at[k])
        block = x.at[k, core, :, :, span[k]]
        sends.append(send(block, block, b_s.at[k], b_r.at[k], {"expert": sibling}))

    def s_up(k):
        start, w = chunks[k]
        arrived(x.at[k, 1 - core, :, :, span[k]], b_r.at[k])
        if k == 0:
            loads[1].wait()
            loads[2].wait()
        rows = x[k].reshape(2 * n_e * HALF, CHUNK)[:, 0:w]
        g = jnp.dot(rows, wg[start:start + w, :], preferred_element_type=f32)
        u = jnp.dot(rows, wu[start:start + w, :], preferred_element_type=f32)
        if k == 0:
            acc_g[...] = g
            acc_u[...] = u
        else:
            acc_g[...] += g
            acc_u[...] += u

    def skewed(stages):
        for t in range(n_c + len(stages) - 1):
            for i, stage in enumerate(stages):
                if 0 <= t - i < n_c:
                    stage(t - i)

    skewed([s_near, s_far, s_swap, s_up])

    arrived(gb.at[:, pl.ds(0, n_e - 1)], gb_r)
    g_lane = lax.broadcasted_iota(jnp.int32, gb.shape, 3)
    gw = jnp.sum(jnp.where(g_lane == me, gb[...], 0.0), axis=3, keepdims=True)
    gw = gw.reshape(2 * n_e * HALF, 1)
    gate = acc_g[...]
    hid[...] = ((acc_u[...] + 1.0) * gate * jax.nn.sigmoid(1.702 * gate) * gw).astype(bf16)
    loads[3].wait()

    def s_down(k):
        start, w = chunks[k]
        part = jnp.dot(hid[...], wd[:, start:start + w], preferred_element_type=f32).astype(bf16)
        ob[k, :, :, :, 0:w] = part.reshape(2, n_e, HALF, w)
        sends.append(send(
            ob.at[k, 1 - core, :, :, span[k]], rb.at[k, :, :, span[k]],
            d_s.at[k], d_r.at[k], {"expert": sibling},
        ))

    def s_pair(k):
        arrived(rb.at[k, :, :, span[k]], d_r.at[k])
        sb[k] = (ob[k, core].astype(f32) + rb[k].astype(f32)).astype(bf16)
        rr[k, me] = sb[k, me]
        for r in range(1, n_e):
            to = lax.rem(me + r, n_e)
            sends.append(send(
                sb.at[k, to, :, span[k]], rr.at[k, me, :, span[k]],
                e_s.at[k, r - 1], e_r.at[k], {"expert": to},
            ))

    def s_sum(k):
        arrived(rr.at[k, pl.ds(0, n_e - 1), :, span[k]], e_r.at[k])
        halves = [
            sum(rr[k, 2 * j + h].astype(f32) for j in range(n_e // 2)) for h in range(2)
        ]
        ret[k, 0:HALF] = halves[0].astype(bf16)
        ret[k, HALF:2 * HALF] = halves[1].astype(bf16)

    def s_near2(k):
        near(k, *line_out)

    def s_far2(k):
        start, w = chunks[k]
        mixture = far(k, *line_out)[:, 0:w]
        spread = jnp.dot(spread_pick, mixture, preferred_element_type=f32)
        out_ref[:, start:start + w] = (
            tokens[:, start:start + w].astype(f32) + keep_col * spread
        ).astype(bf16)

    skewed([s_down, s_pair, s_sum, s_near2, s_far2])

    for copy in sends:
        copy.wait_send()
    for k in range(n_c):
        line_drain(k, zsend, z_s)
        line_drain(k, zsend2, z2_s)


def fused(tokens, passes, keep, gain, routes, gates, wg, wu, wd):
    n_z, n_e = lax.axis_size("dp"), lax.axis_size("expert")
    t_tok, width = tokens.shape
    seq_keep = routes.shape[1]
    hidden = wg.shape[2]
    n_c = len(chunks_of(width))
    bf16, f32 = jnp.bfloat16, jnp.float32
    vmem = pl.BlockSpec(memory_space=pltpu.VMEM)
    hbm = pl.BlockSpec(memory_space=pl.ANY)
    dma = pltpu.SemaphoreType.DMA
    rows = n_e * seq_keep
    line = pltpu.VMEM((2, n_c, seq_keep, CHUNK), bf16)
    single = pltpu.VMEM((n_c, seq_keep, CHUNK), bf16)
    block = pltpu.VMEM((n_c, n_e, HALF, CHUNK), bf16)
    both = pltpu.VMEM((n_c, 2, n_e, HALF, CHUNK), bf16)
    return pl.pallas_call(
        fused_kernel,
        out_shape=jax.ShapeDtypeStruct((t_tok, width), bf16),
        in_specs=[hbm, vmem, vmem, vmem, vmem, vmem, hbm, hbm, hbm],
        out_specs=vmem,
        scratch_shapes=[
            pltpu.VMEM((t_tok, width), bf16),
            pltpu.VMEM(wg.shape[1:], bf16),
            pltpu.VMEM(wu.shape[1:], bf16),
            pltpu.VMEM(wd.shape[1:], bf16),
            pltpu.VMEM((n_z, 8, t_tok), f32),
            pltpu.VMEM((2, n_e, HALF, LANES), f32),
            single, line, line,
            pltpu.VMEM((n_c, 2, HALF, CHUNK), bf16),
            both,
            pltpu.VMEM((rows, hidden), f32),
            pltpu.VMEM((rows, hidden), f32),
            pltpu.VMEM((rows, hidden), bf16),
            both, block, block, block,
            single, line, line,
            dma((4,)), dma((n_z - 1,)), dma, dma((n_e - 1,)), dma,
            dma((2, n_c)), dma((2, n_c)),
            dma((n_c, n_e - 1)), dma((n_c,)),
            dma((n_c,)), dma((n_c,)),
            dma((n_c,)), dma((n_c,)),
            dma((n_c, n_e - 1)), dma((n_c,)),
            dma((2, n_c)), dma((2, n_c)),
        ],
        compiler_params=pltpu.CompilerParams(
            collective_id=0, has_side_effects=True, vmem_limit_bytes=48 * 1024 * 1024
        ),
    )(
        tokens, passes.reshape(1, t_tok), keep.reshape(1, t_tok), gain.reshape(1, width),
        routes[0], gates[0], wg[0], wu[0], wd[0],
    )


def rescaled_entries(rows_in, gain_row):
    scaling = lax.rsqrt(jnp.mean(rows_in * rows_in, axis=-1, keepdims=True) + 1e-05)
    return (rows_in * scaling * gain_row).astype(jnp.bfloat16)


def local(
    tokens, passes_through, keep_weight, norm_gain, routes, gate_values, w_gate, w_up, w_down
):
    piece_vectors, feature_width = tokens.shape
    batch_clusters = lax.axis_size("dp")
    experts = lax.axis_size("expert")
    most_local = 3 * (piece_vectors // 16)
    seq_keep = routes.shape[1]
    top_count = routes.shape[2]
    capacity = max(2, batch_clusters * (piece_vectors // 16) * top_count // experts * 5 // 4)
    ranking = jnp.cumsum(passes_through) - 1
    picker = (
        (ranking[None, :] == jnp.arange(most_local)[:, None]) & (passes_through[None, :] == 1)
    ).astype(jnp.bfloat16)
    compact = jnp.dot(picker, tokens, preferred_element_type=jnp.float32)
    normalized_rows = rescaled_entries(compact, norm_gain)
    remaining_total = jnp.sum(passes_through)
    gathered, counts_all = (
        lax.all_gather(normalized_rows, "dp", axis=0, tiled=True),
        lax.all_gather(remaining_total.reshape(1), "dp", axis=0, tiled=True),
    )
    offsets = jnp.cumsum(counts_all) - counts_all
    within = jnp.arange(most_local, dtype=jnp.int32)
    token_positions = (offsets[:, None] + within[None, :]).reshape(-1)
    valid_mask = (within[None, :] < counts_all[:, None]).reshape(-1)
    order_pick = (
        (token_positions[None, :] == jnp.arange(seq_keep)[:, None]) & valid_mask[None, :]
    ).astype(jnp.bfloat16)
    column_rows = jnp.dot(order_pick, gathered, preferred_element_type=jnp.float32).astype(
        jnp.bfloat16
    )
    flat_routes = routes.reshape(-1)
    onehot = (flat_routes[:, None] == jnp.arange(experts)[None, :]).astype(jnp.int32)
    slot_rank = jnp.sum((jnp.cumsum(onehot, axis=0) - onehot) * onehot, axis=1)
    targets = (flat_routes * capacity + slot_rank).reshape(seq_keep, top_count)
    slot_ids = jnp.arange(experts * capacity)
    dispatch = jnp.any(targets[None, :, :] == slot_ids[:, None, None], axis=-1).astype(jnp.bfloat16)
    buffer = jnp.dot(dispatch, column_rows, preferred_element_type=jnp.float32).astype(jnp.bfloat16)
    received = lax.all_to_all(buffer, "expert", split_axis=0, concat_axis=0, tiled=True)
    gate_proj = jnp.dot(received, w_gate[0], preferred_element_type=jnp.float32)
    up_proj = jnp.dot(received, w_up[0], preferred_element_type=jnp.float32)
    hidden = ((up_proj + 1.0) * gate_proj * jax.nn.sigmoid(1.702 * gate_proj)).astype(jnp.bfloat16)
    partials = jnp.dot(hidden, w_down[0], preferred_element_type=jnp.float32)
    summed = lax.psum_scatter(partials.astype(jnp.bfloat16), "dp", scatter_dimension=1, tiled=True)
    returned = lax.all_to_all(summed, "expert", split_axis=0, concat_axis=0, tiled=True)
    combine_weights = jnp.sum(
        (targets[:, :, None] == slot_ids[None, None, :]).astype(jnp.float32)
        * gate_values[0][:, :, None],
        axis=1,
    )
    mixture = jnp.dot(
        combine_weights, returned.astype(jnp.float32), precision=lax.Precision.HIGHEST
    )
    moe_rows = mixture.astype(jnp.bfloat16)
    owned = jnp.dot(order_pick.T, moe_rows, preferred_element_type=jnp.float32).astype(jnp.bfloat16)
    own_rows = lax.all_to_all(owned, "dp", split_axis=0, concat_axis=1, tiled=True)
    spread = jnp.dot(picker.T, own_rows, preferred_element_type=jnp.float32)
    result = tokens.astype(jnp.float32) + keep_weight[:, None] * spread
    return result.astype(jnp.bfloat16)


def layer(tokens, passes_through, keep_weight, norm_gain, routes, gate_values, w_gate, w_up, w_down):
    lines, experts = lax.axis_size("dp"), lax.axis_size("expert")
    fits = lines == 4 and experts % 2 == 0 and experts * routes.shape[1] <= 512
    step = fused if fits and routes.shape[1] == 2 * HALF and experts <= LANES else local
    return step(
        tokens, passes_through, keep_weight, norm_gain, routes, gate_values, w_gate, w_up, w_down
    )


def solution(mesh):
    return jax.shard_map(
        layer,
        mesh=mesh,
        in_specs=(
            P(("expert", "dp"), None),
            P(("expert", "dp")),
            P(("expert", "dp")),
            P(),
            P("expert", None, None),
            P("expert", None, None),
            P("expert", None, "dp"),
            P("expert", None, "dp"),
            P("expert", "dp", None),
        ),
        out_specs=P(("expert", "dp"), None),
        check_vma=False,
    )
```

```python
import jax
import jax.numpy as jnp
from jax import lax
from jax.experimental import pallas as pl
from jax.experimental.pallas import tpu as pltpu
from jax.sharding import PartitionSpec as P

CHUNK = 1536
LANES = 128
HALF = 16
NT = (((1,), (1,)), ((), ()))
TN = (((0,), (0,)), ((), ()))


def chunks_of(width):
    starts = list(range(0, width, CHUNK))
    return [(s, min(CHUNK, width - s)) for s in starts]


def fused_kernel(
    tokens_hbm, passes_ref, keep_ref, gain_ref, routes_ref, gates_ref, wg_hbm, wu_hbm, wd_hbm,
    out_ref,
    tokens, wg, wu, wd, cnt, gb, own, zin, zsend, tot, x, acc_g, acc_u, hid, ob, rb, sb, rr,
    ret, zin2, zsend2,
    ld_sem, cnt_s, cnt_r, gb_s, gb_r, z_s, z_r, a_s, a_r, b_s, b_r, d_s, d_r, e_s, e_r, z2_s, z2_r,
):
    z, me = lax.axis_index("dp"), lax.axis_index("expert")
    n_z, n_e = lax.axis_size("dp"), lax.axis_size("expert")
    width = tokens.shape[0]
    chunks = chunks_of(width)
    n_c = len(chunks)
    span = [pl.ds(0, -(-w // LANES) * LANES) for _, w in chunks]
    core = lax.rem(me, 2)
    sibling = me + 1 - 2 * core
    low = z < 2
    edge = jnp.logical_or(z == 0, z == n_z - 1)
    middle = jnp.logical_not(edge)
    inward = jnp.where(low, z + 1, z - 1)
    outward = jnp.where(z == 1, 0, n_z - 1)
    lands = jnp.where(edge, 0, 1)
    f32, bf16 = jnp.float32, jnp.bfloat16

    loads = [
        pltpu.make_async_copy(tokens_hbm, tokens, ld_sem.at[0]),
        pltpu.make_async_copy(wg_hbm, wg, ld_sem.at[1]),
        pltpu.make_async_copy(wu_hbm, wu, ld_sem.at[2]),
        pltpu.make_async_copy(wd_hbm, wd, ld_sem.at[3]),
    ]
    for load in loads:
        load.start()

    barrier = pltpu.get_barrier_semaphore()
    for r in range(1, n_z):
        pl.semaphore_signal(barrier, inc=1, device_id={"dp": lax.rem(z + r, n_z)})
    for r in range(1, n_e):
        pl.semaphore_signal(barrier, inc=1, device_id={"expert": lax.rem(me + r, n_e)})

    flags = passes_ref[...].astype(f32)
    t_tok = flags.shape[1]
    sub = lax.broadcasted_iota(jnp.int32, (t_tok, t_tok), 0)
    lane = lax.broadcasted_iota(jnp.int32, (t_tok, t_tok), 1)
    wide = jnp.broadcast_to(flags, (t_tok, t_tok))
    flag_col = jnp.sum(jnp.where(lane == sub, wide, 0.0), axis=1, keepdims=True)
    rank_row = jnp.sum(jnp.where(sub <= lane, flag_col, 0.0), axis=0, keepdims=True) - 1.0

    cnt[z] = jnp.broadcast_to(flags, cnt.shape[1:])
    top, seq_keep = routes_ref.shape
    diagonal = lax.broadcasted_iota(jnp.int32, (seq_keep, seq_keep), 0) == (
        lax.broadcasted_iota(jnp.int32, (seq_keep, seq_keep), 1)
    )

    def as_column(row):
        square = jnp.broadcast_to(row, (seq_keep, seq_keep))
        return jnp.sum(jnp.where(diagonal, square, jnp.zeros_like(square)), axis=1, keepdims=True)

    e_lane = lax.broadcasted_iota(jnp.int32, (seq_keep, LANES), 1)
    weights = jnp.zeros((seq_keep, LANES), f32)
    for k in range(top):
        weights += jnp.where(
            as_column(routes_ref[k:k + 1, :].astype(f32)) == e_lane.astype(f32),
            as_column(gates_ref[k:k + 1, :]), 0.0,
        )
    gb[:, me] = weights.reshape(2, HALF, LANES)

    pl.semaphore_wait(barrier, n_z - 1 + n_e - 1)
    sends = []

    def send(src, dst, ssem, rsem, device):
        copy = pltpu.make_async_remote_copy(
            src_ref=src, dst_ref=dst, send_sem=ssem, recv_sem=rsem, device_id=device,
            device_id_type=pl.DeviceIdType.MESH,
        )
        copy.start()
        return copy

    def arrived(ref, sem):
        pltpu.make_async_copy(ref, ref, sem).wait()

    for r in range(1, n_z):
        sends.append(send(cnt.at[z], cnt.at[z], cnt_s.at[r - 1], cnt_r, {"dp": lax.rem(z + r, n_z)}))
    for r in range(1, n_e):
        sends.append(
            send(gb.at[:, me], gb.at[:, me], gb_s.at[r - 1], gb_r, {"expert": lax.rem(me + r, n_e)})
        )

    loads[0].wait()
    arrived(cnt.at[pl.ds(0, n_z - 1)], cnt_r)
    offset = jnp.zeros((1, 1), f32)
    for other in range(n_z):
        total = jnp.sum(cnt[other, 0:1, :], axis=1, keepdims=True)
        offset += jnp.where(other < z, total, 0.0)
    s_sub = lax.broadcasted_iota(jnp.int32, (seq_keep, t_tok), 0).astype(f32)
    picker = jnp.where((rank_row + offset == s_sub) & (flags > 0.5), 1.0, 0.0).astype(bf16)
    compact = lax.dot_general(picker, tokens[...], NT, preferred_element_type=f32)
    scaling = lax.rsqrt(jnp.sum(compact * compact, axis=1, keepdims=True) * (1.0 / width) + 1e-05)
    normed = (compact * scaling * gain_ref[...]).astype(bf16)

    @pl.when(edge)
    def _():
        zin[0] = jnp.zeros_like(zin[0])
        zin2[0] = jnp.zeros_like(zin2[0])

    for k, (start, w) in enumerate(chunks):
        own[k, :, 0:w] = normed[:, start:start + w]

    def line_copy(src, dst, k, which, s_sems, r_sems, device):
        return pltpu.make_async_remote_copy(
            src_ref=src, dst_ref=dst, send_sem=s_sems.at[which, k], recv_sem=r_sems,
            device_id={"dp": device}, device_id_type=pl.DeviceIdType.MESH,
        )

    def near(k, mine, into, out, s_sems, r_sems):
        @pl.when(middle)
        def _():
            arrived(into.at[0, k, :, span[k]], r_sems.at[0, k])

        out[0, k] = (mine[k].astype(f32) + into[0, k].astype(f32)).astype(bf16)
        line_copy(
            out.at[0, k, :, span[k]], into.at[lands, k, :, span[k]], k, 0, s_sems,
            r_sems.at[lands, k], inward,
        ).start()

    def far(k, mine, into, out, s_sems, r_sems):
        arrived(into.at[1, k, :, span[k]], r_sems.at[1, k])
        part = mine[k].astype(f32) + into[1, k].astype(f32)

        @pl.when(middle)
        def _():
            out[1, k] = part.astype(bf16)
            line_copy(
                out.at[1, k, :, span[k]], into.at[1, k, :, span[k]], k, 1, s_sems,
                r_sems.at[1, k], outward,
            ).start()

        return (part + into[0, k].astype(f32)).astype(bf16)

    def line_drain(k, out, s_sems):
        arrived(out.at[0, k, :, span[k]], s_sems.at[0, k])

        @pl.when(middle)
        def _():
            arrived(out.at[1, k, :, span[k]], s_sems.at[1, k])

    line_in = (own, zin, zsend, z_s, z_r)
    line_out = (ret, zin2, zsend2, z2_s, z2_r)

    def s_near(k):
        near(k, *line_in)

    def s_far(k):
        tot[k] = far(k, *line_in).reshape(2, HALF, CHUNK)
        x[k, core, me] = tot[k, core]
        for r in range(1, n_e):
            to = lax.rem(me + r, n_e)
            side = lax.rem(to, 2)
            sends.append(send(
                tot.at[k, side, :, span[k]], x.at[k, side, me, :, span[k]],
                a_s.at[k, r - 1], a_r.at[k], {"expert": to},
            ))

    def s_swap(k):
        arrived(x.at[k, core, pl.ds(0, n_e - 1), :, span[k]], a_r.at[k])
        block = x.at[k, core, :, :, span[k]]
        sends.append(send(block, block, b_s.at[k], b_r.at[k], {"expert": sibling}))

    def s_up(k):
        start, w = chunks[k]
        arrived(x.at[k, 1 - core, :, :, span[k]], b_r.at[k])
        if k == 0:
            loads[1].wait()
            loads[2].wait()
        rows = x[k].reshape(2 * n_e * HALF, CHUNK)[:, 0:w]
        g = lax.dot_general(rows, wg[:, start:start + w], NT, preferred_element_type=f32)
        u = lax.dot_general(rows, wu[:, start:start + w], NT, preferred_element_type=f32)
        if k == 0:
            acc_g[...] = g
            acc_u[...] = u
        else:
            acc_g[...] += g
            acc_u[...] += u

    def skewed(stages):
        for t in range(n_c + len(stages) - 1):
            for i, stage in enumerate(stages):
                if 0 <= t - i < n_c:
                    stage(t - i)

    skewed([s_near, s_far, s_swap, s_up])

    arrived(gb.at[:, pl.ds(0, n_e - 1)], gb_r)
    g_lane = lax.broadcasted_iota(jnp.int32, gb.shape, 3)
    gw = jnp.sum(jnp.where(g_lane == me, gb[...], 0.0), axis=3, keepdims=True)
    gw = gw.reshape(2 * n_e * HALF, 1)
    gate = acc_g[...]
    hid[...] = ((acc_u[...] + 1.0) * gate * jax.nn.sigmoid(1.702 * gate) * gw).astype(bf16)
    loads[3].wait()

    def s_down(k):
        start, w = chunks[k]
        part = jnp.dot(hid[...], wd[:, start:start + w], preferred_element_type=f32).astype(bf16)
        ob[k, :, :, :, 0:w] = part.reshape(2, n_e, HALF, w)
        sends.append(send(
            ob.at[k, 1 - core, :, :, span[k]], rb.at[k, :, :, span[k]],
            d_s.at[k], d_r.at[k], {"expert": sibling},
        ))

    def s_pair(k):
        arrived(rb.at[k, :, :, span[k]], d_r.at[k])
        sb[k] = (ob[k, core].astype(f32) + rb[k].astype(f32)).astype(bf16)
        rr[k, me] = sb[k, me]
        for r in range(1, n_e):
            to = lax.rem(me + r, n_e)
            sends.append(send(
                sb.at[k, to, :, span[k]], rr.at[k, me, :, span[k]],
                e_s.at[k, r - 1], e_r.at[k], {"expert": to},
            ))

    def s_sum(k):
        arrived(rr.at[k, pl.ds(0, n_e - 1), :, span[k]], e_r.at[k])
        halves = [
            sum(rr[k, 2 * j + h].astype(f32) for j in range(n_e // 2)) for h in range(2)
        ]
        ret[k, 0:HALF] = halves[0].astype(bf16)
        ret[k, HALF:2 * HALF] = halves[1].astype(bf16)

    def s_near2(k):
        near(k, *line_out)

    def s_far2(k):
        start, w = chunks[k]
        mixture = far(k, *line_out)[:, 0:w]
        spread = lax.dot_general(mixture, picker, TN, preferred_element_type=f32)
        out_ref[start:start + w, :] = (
            tokens[start:start + w, :].astype(f32) + keep_ref[...] * spread
        ).astype(bf16)

    skewed([s_down, s_pair, s_sum, s_near2, s_far2])

    for copy in sends:
        copy.wait_send()
    for k in range(n_c):
        line_drain(k, zsend, z_s)
        line_drain(k, zsend2, z2_s)


def fused(tokens, passes, keep, gain, routes, gates, wg, wu, wd):
    n_z, n_e = lax.axis_size("dp"), lax.axis_size("expert")
    t_tok, width = tokens.shape
    seq_keep = routes.shape[1]
    hidden = wg.shape[2]
    turned = lambda w: jnp.swapaxes(w[0], 0, 1)
    n_c = len(chunks_of(width))
    bf16, f32 = jnp.bfloat16, jnp.float32
    vmem = pl.BlockSpec(memory_space=pltpu.VMEM)
    hbm = pl.BlockSpec(memory_space=pl.ANY)
    dma = pltpu.SemaphoreType.DMA
    rows = n_e * seq_keep
    line = pltpu.VMEM((2, n_c, seq_keep, CHUNK), bf16)
    single = pltpu.VMEM((n_c, seq_keep, CHUNK), bf16)
    block = pltpu.VMEM((n_c, n_e, HALF, CHUNK), bf16)
    both = pltpu.VMEM((n_c, 2, n_e, HALF, CHUNK), bf16)
    return pl.pallas_call(
        fused_kernel,
        out_shape=jax.ShapeDtypeStruct((width, t_tok), bf16),
        in_specs=[hbm, vmem, vmem, vmem, vmem, vmem, hbm, hbm, hbm],
        out_specs=vmem,
        scratch_shapes=[
            pltpu.VMEM((width, t_tok), bf16),
            pltpu.VMEM((hidden, width), bf16),
            pltpu.VMEM((hidden, width), bf16),
            pltpu.VMEM(wd.shape[1:], bf16),
            pltpu.VMEM((n_z, 8, t_tok), f32),
            pltpu.VMEM((2, n_e, HALF, LANES), f32),
            single, line, line,
            pltpu.VMEM((n_c, 2, HALF, CHUNK), bf16),
            both,
            pltpu.VMEM((rows, hidden), f32),
            pltpu.VMEM((rows, hidden), f32),
            pltpu.VMEM((rows, hidden), bf16),
            both, block, block, block,
            single, line, line,
            dma((4,)), dma((n_z - 1,)), dma, dma((n_e - 1,)), dma,
            dma((2, n_c)), dma((2, n_c)),
            dma((n_c, n_e - 1)), dma((n_c,)),
            dma((n_c,)), dma((n_c,)),
            dma((n_c,)), dma((n_c,)),
            dma((n_c, n_e - 1)), dma((n_c,)),
            dma((2, n_c)), dma((2, n_c)),
        ],
        compiler_params=pltpu.CompilerParams(
            collective_id=0, has_side_effects=True, vmem_limit_bytes=58 * 1024 * 1024
        ),
    )(
        tokens.T, passes.reshape(1, t_tok), keep.reshape(1, t_tok), gain.reshape(1, width),
        turned(routes), turned(gates), turned(wg), turned(wu), wd[0],
    ).T


def rescaled_entries(rows_in, gain_row):
    scaling = lax.rsqrt(jnp.mean(rows_in * rows_in, axis=-1, keepdims=True) + 1e-05)
    return (rows_in * scaling * gain_row).astype(jnp.bfloat16)


def local(
    tokens, passes_through, keep_weight, norm_gain, routes, gate_values, w_gate, w_up, w_down
):
    piece_vectors, feature_width = tokens.shape
    batch_clusters = lax.axis_size("dp")
    experts = lax.axis_size("expert")
    most_local = 3 * (piece_vectors // 16)
    seq_keep = routes.shape[1]
    top_count = routes.shape[2]
    capacity = max(2, batch_clusters * (piece_vectors // 16) * top_count // experts * 5 // 4)
    ranking = jnp.cumsum(passes_through) - 1
    picker = (
        (ranking[None, :] == jnp.arange(most_local)[:, None]) & (passes_through[None, :] == 1)
    ).astype(jnp.bfloat16)
    compact = jnp.dot(picker, tokens, preferred_element_type=jnp.float32)
    normalized_rows = rescaled_entries(compact, norm_gain)
    remaining_total = jnp.sum(passes_through)
    gathered, counts_all = (
        lax.all_gather(normalized_rows, "dp", axis=0, tiled=True),
        lax.all_gather(remaining_total.reshape(1), "dp", axis=0, tiled=True),
    )
    offsets = jnp.cumsum(counts_all) - counts_all
    within = jnp.arange(most_local, dtype=jnp.int32)
    token_positions = (offsets[:, None] + within[None, :]).reshape(-1)
    valid_mask = (within[None, :] < counts_all[:, None]).reshape(-1)
    order_pick = (
        (token_positions[None, :] == jnp.arange(seq_keep)[:, None]) & valid_mask[None, :]
    ).astype(jnp.bfloat16)
    column_rows = jnp.dot(order_pick, gathered, preferred_element_type=jnp.float32).astype(
        jnp.bfloat16
    )
    flat_routes = routes.reshape(-1)
    onehot = (flat_routes[:, None] == jnp.arange(experts)[None, :]).astype(jnp.int32)
    slot_rank = jnp.sum((jnp.cumsum(onehot, axis=0) - onehot) * onehot, axis=1)
    targets = (flat_routes * capacity + slot_rank).reshape(seq_keep, top_count)
    slot_ids = jnp.arange(experts * capacity)
    dispatch = jnp.any(targets[None, :, :] == slot_ids[:, None, None], axis=-1).astype(jnp.bfloat16)
    buffer = jnp.dot(dispatch, column_rows, preferred_element_type=jnp.float32).astype(jnp.bfloat16)
    received = lax.all_to_all(buffer, "expert", split_axis=0, concat_axis=0, tiled=True)
    gate_proj = jnp.dot(received, w_gate[0], preferred_element_type=jnp.float32)
    up_proj = jnp.dot(received, w_up[0], preferred_element_type=jnp.float32)
    hidden = ((up_proj + 1.0) * gate_proj * jax.nn.sigmoid(1.702 * gate_proj)).astype(jnp.bfloat16)
    partials = jnp.dot(hidden, w_down[0], preferred_element_type=jnp.float32)
    summed = lax.psum_scatter(partials.astype(jnp.bfloat16), "dp", scatter_dimension=1, tiled=True)
    returned = lax.all_to_all(summed, "expert", split_axis=0, concat_axis=0, tiled=True)
    combine_weights = jnp.sum(
        (targets[:, :, None] == slot_ids[None, None, :]).astype(jnp.float32)
        * gate_values[0][:, :, None],
        axis=1,
    )
    mixture = jnp.dot(
        combine_weights, returned.astype(jnp.float32), precision=lax.Precision.HIGHEST
    )
    moe_rows = mixture.astype(jnp.bfloat16)
    owned = jnp.dot(order_pick.T, moe_rows, preferred_element_type=jnp.float32).astype(jnp.bfloat16)
    own_rows = lax.all_to_all(owned, "dp", split_axis=0, concat_axis=1, tiled=True)
    spread = jnp.dot(picker.T, own_rows, preferred_element_type=jnp.float32)
    result = tokens.astype(jnp.float32) + keep_weight[:, None] * spread
    return result.astype(jnp.bfloat16)


def layer(tokens, passes_through, keep_weight, norm_gain, routes, gate_values, w_gate, w_up, w_down):
    lines, experts = lax.axis_size("dp"), lax.axis_size("expert")
    fits = lines == 4 and experts % 2 == 0 and experts * routes.shape[1] <= 512
    step = fused if fits and routes.shape[1] == 2 * HALF and experts <= LANES else local
    return step(
        tokens, passes_through, keep_weight, norm_gain, routes, gate_values, w_gate, w_up, w_down
    )


def solution(mesh):
    return jax.shard_map(
        layer,
        mesh=mesh,
        in_specs=(
            P(("expert", "dp"), None),
            P(("expert", "dp")),
            P(("expert", "dp")),
            P(),
            P("expert", None, None),
            P("expert", None, None),
            P("expert", None, "dp"),
            P("expert", None, "dp"),
            P("expert", "dp", None),
        ),
        out_specs=P(("expert", "dp"), None),
        check_vma=False,
    )
```

```python
import jax
import jax.numpy as jnp
from jax import lax
from jax.experimental import pallas as pl
from jax.experimental.pallas import tpu as pltpu
from jax.sharding import PartitionSpec as P

CHUNK = 1536
LANES = 128
HALF = 16
NT = (((1,), (1,)), ((), ()))
TN = (((0,), (0,)), ((), ()))


def chunks_of(width):
    starts = list(range(0, width, CHUNK))
    return [(s, min(CHUNK, width - s)) for s in starts]


def fused_kernel(
    tokens_hbm, passes_ref, keep_ref, gain_ref, routes_ref, gates_ref, wg_hbm, wu_hbm, wd_hbm,
    out_ref,
    tokens, wg, wu, wd, cnt, gb, own, zin, zsend, tot, x, acc_g, acc_u, hid, ob, rb, sb, rr,
    ret, zin2, zsend2,
    ld_sem, cnt_s, cnt_r, gb_s, gb_r, z_s, z_r, a_s, a_r, b_s, b_r, d_s, d_r, e_s, e_r, z2_s, z2_r,
):
    z, me = lax.axis_index("dp"), lax.axis_index("expert")
    n_z, n_e = lax.axis_size("dp"), lax.axis_size("expert")
    width = tokens.shape[0]
    chunks = chunks_of(width)
    n_c = len(chunks)
    span = [pl.ds(0, -(-w // LANES) * LANES) for _, w in chunks]
    core = lax.rem(me, 2)
    sibling = me + 1 - 2 * core
    low = z < 2
    edge = jnp.logical_or(z == 0, z == n_z - 1)
    middle = jnp.logical_not(edge)
    inward = jnp.where(low, z + 1, z - 1)
    outward = jnp.where(z == 1, 0, n_z - 1)
    lands = jnp.where(edge, 0, 1)
    f32, bf16 = jnp.float32, jnp.bfloat16

    loads = [
        pltpu.make_async_copy(tokens_hbm, tokens, ld_sem.at[0]),
        pltpu.make_async_copy(wg_hbm, wg, ld_sem.at[1]),
        pltpu.make_async_copy(wu_hbm, wu, ld_sem.at[2]),
        pltpu.make_async_copy(wd_hbm, wd, ld_sem.at[3]),
    ]
    for load in loads:
        load.start()

    barrier = pltpu.get_barrier_semaphore()
    for r in range(1, n_z):
        pl.semaphore_signal(barrier, inc=1, device_id={"dp": lax.rem(z + r, n_z)})
    for r in range(1, n_e):
        pl.semaphore_signal(barrier, inc=1, device_id={"expert": lax.rem(me + r, n_e)})

    flags = passes_ref[...].astype(f32)
    t_tok = flags.shape[1]
    sub = lax.broadcasted_iota(jnp.int32, (t_tok, t_tok), 0)
    lane = lax.broadcasted_iota(jnp.int32, (t_tok, t_tok), 1)
    wide = jnp.broadcast_to(flags, (t_tok, t_tok))
    flag_col = jnp.sum(jnp.where(lane == sub, wide, 0.0), axis=1, keepdims=True)
    rank_row = jnp.sum(jnp.where(sub <= lane, flag_col, 0.0), axis=0, keepdims=True) - 1.0

    cnt[z] = jnp.broadcast_to(flags, cnt.shape[1:])
    top, seq_keep = routes_ref.shape
    diagonal = lax.broadcasted_iota(jnp.int32, (seq_keep, seq_keep), 0) == (
        lax.broadcasted_iota(jnp.int32, (seq_keep, seq_keep), 1)
    )

    def as_column(row):
        square = jnp.broadcast_to(row, (seq_keep, seq_keep))
        return jnp.sum(jnp.where(diagonal, square, jnp.zeros_like(square)), axis=1, keepdims=True)

    e_lane = lax.broadcasted_iota(jnp.int32, (seq_keep, LANES), 1)
    weights = jnp.zeros((seq_keep, LANES), f32)
    for k in range(top):
        weights += jnp.where(
            as_column(routes_ref[k:k + 1, :].astype(f32)) == e_lane.astype(f32),
            as_column(gates_ref[k:k + 1, :]), 0.0,
        )
    gb[:, me] = weights.reshape(2, HALF, LANES)

    pl.semaphore_wait(barrier, n_z - 1 + n_e - 1)
    sends = []

    def send(src, dst, ssem, rsem, device):
        copy = pltpu.make_async_remote_copy(
            src_ref=src, dst_ref=dst, send_sem=ssem, recv_sem=rsem, device_id=device,
            device_id_type=pl.DeviceIdType.MESH,
        )
        copy.start()
        return copy

    def arrived(ref, sem):
        pltpu.make_async_copy(ref, ref, sem).wait()

    for r in range(1, n_z):
        sends.append(send(cnt.at[z], cnt.at[z], cnt_s.at[r - 1], cnt_r, {"dp": lax.rem(z + r, n_z)}))
    for r in range(1, n_e):
        sends.append(
            send(gb.at[:, me], gb.at[:, me], gb_s.at[r - 1], gb_r, {"expert": lax.rem(me + r, n_e)})
        )

    loads[0].wait()
    arrived(cnt.at[pl.ds(0, n_z - 1)], cnt_r)
    offset = jnp.zeros((1, 1), f32)
    for other in range(n_z):
        total = jnp.sum(cnt[other, 0:1, :], axis=1, keepdims=True)
        offset += jnp.where(other < z, total, 0.0)
    s_sub = lax.broadcasted_iota(jnp.int32, (seq_keep, t_tok), 0).astype(f32)
    picker = jnp.where((rank_row + offset == s_sub) & (flags > 0.5), 1.0, 0.0).astype(bf16)
    compact = lax.dot_general(picker, tokens[...], NT, preferred_element_type=f32)
    scaling = lax.rsqrt(jnp.sum(compact * compact, axis=1, keepdims=True) * (1.0 / width) + 1e-05)
    normed = (compact * scaling * gain_ref[...]).astype(bf16)

    @pl.when(edge)
    def _():
        zin[0] = jnp.zeros_like(zin[0])
        zin2[0] = jnp.zeros_like(zin2[0])

    for k, (start, w) in enumerate(chunks):
        own[k, :, 0:w] = normed[:, start:start + w]

    def line_copy(src, dst, k, which, s_sems, r_sems, device):
        return pltpu.make_async_remote_copy(
            src_ref=src, dst_ref=dst, send_sem=s_sems.at[which, k], recv_sem=r_sems,
            device_id={"dp": device}, device_id_type=pl.DeviceIdType.MESH,
        )

    def near(k, mine, into, out, s_sems, r_sems):
        @pl.when(middle)
        def _():
            arrived(into.at[0, k, :, span[k]], r_sems.at[0, k])

        out[0, k] = (mine[k].astype(f32) + into[0, k].astype(f32)).astype(bf16)
        line_copy(
            out.at[0, k, :, span[k]], into.at[lands, k, :, span[k]], k, 0, s_sems,
            r_sems.at[lands, k], inward,
        ).start()

    def far(k, mine, into, out, s_sems, r_sems):
        arrived(into.at[1, k, :, span[k]], r_sems.at[1, k])
        part = mine[k].astype(f32) + into[1, k].astype(f32)

        @pl.when(middle)
        def _():
            out[1, k] = part.astype(bf16)
            line_copy(
                out.at[1, k, :, span[k]], into.at[1, k, :, span[k]], k, 1, s_sems,
                r_sems.at[1, k], outward,
            ).start()

        return (part + into[0, k].astype(f32)).astype(bf16)

    def line_drain(k, out, s_sems):
        arrived(out.at[0, k, :, span[k]], s_sems.at[0, k])

        @pl.when(middle)
        def _():
            arrived(out.at[1, k, :, span[k]], s_sems.at[1, k])

    line_in = (own, zin, zsend, z_s, z_r)
    line_out = (ret, zin2, zsend2, z2_s, z2_r)

    def s_near(k):
        near(k, *line_in)

    def s_far(k):
        tot[k] = far(k, *line_in).reshape(2, HALF, CHUNK)
        x[k, core, me] = tot[k, core]
        for r in range(1, n_e):
            to = lax.rem(me + r, n_e)
            side = lax.rem(to, 2)
            sends.append(send(
                tot.at[k, side, :, span[k]], x.at[k, side, me, :, span[k]],
                a_s.at[k, r - 1], a_r.at[k], {"expert": to},
            ))

    def s_swap(k):
        arrived(x.at[k, core, pl.ds(0, n_e - 1), :, span[k]], a_r.at[k])
        block = x.at[k, core, :, :, span[k]]
        sends.append(send(block, block, b_s.at[k], b_r.at[k], {"expert": sibling}))

    def s_up(k):
        start, w = chunks[k]
        arrived(x.at[k, 1 - core, :, :, span[k]], b_r.at[k])
        if k == 0:
            loads[1].wait()
            loads[2].wait()
        rows = x[k].reshape(2 * n_e * HALF, CHUNK)[:, 0:w]
        g = lax.dot_general(rows, wg[:, start:start + w], NT, preferred_element_type=f32)
        u = lax.dot_general(rows, wu[:, start:start + w], NT, preferred_element_type=f32)
        if k == 0:
            acc_g[...] = g
            acc_u[...] = u
        else:
            acc_g[...] += g
            acc_u[...] += u

    def skewed(stages):
        for t in range(n_c + len(stages) - 1):
            for i, stage in enumerate(stages):
                if 0 <= t - i < n_c:
                    stage(t - i)

    skewed([s_near, s_far, s_swap, s_up])

    arrived(gb.at[:, pl.ds(0, n_e - 1)], gb_r)
    g_lane = lax.broadcasted_iota(jnp.int32, gb.shape, 3)
    gw = jnp.sum(jnp.where(g_lane == me, gb[...], 0.0), axis=3, keepdims=True)
    gw = gw.reshape(2 * n_e * HALF, 1)
    gate = acc_g[...]
    hid[...] = ((acc_u[...] + 1.0) * gate * jax.nn.sigmoid(1.702 * gate) * gw).astype(bf16).reshape(hid.shape)
    loads[3].wait()

    def down_half(k, half):
        start, w = chunks[k]
        part = jnp.dot(hid[half], wd[:, start:start + w], preferred_element_type=f32)
        ob[k, half, :, :, 0:w] = part.astype(bf16).reshape(n_e, HALF, w)

    def s_down(k):
        down_half(k, 1 - core)
        sends.append(send(
            ob.at[k, 1 - core, :, :, span[k]], rb.at[k, :, :, span[k]],
            d_s.at[k], d_r.at[k], {"expert": sibling},
        ))

    def s_pair(k):
        down_half(k, core)
        arrived(rb.at[k, :, :, span[k]], d_r.at[k])
        sb[k] = (ob[k, core].astype(f32) + rb[k].astype(f32)).astype(bf16)
        rr[k, me] = sb[k, me]
        for r in range(1, n_e):
            to = lax.rem(me + r, n_e)
            sends.append(send(
                sb.at[k, to, :, span[k]], rr.at[k, me, :, span[k]],
                e_s.at[k, r - 1], e_r.at[k], {"expert": to},
            ))

    def s_sum(k):
        arrived(rr.at[k, pl.ds(0, n_e - 1), :, span[k]], e_r.at[k])
        halves = [
            sum(rr[k, 2 * j + h].astype(f32) for j in range(n_e // 2)) for h in range(2)
        ]
        ret[k, 0:HALF] = halves[0].astype(bf16)
        ret[k, HALF:2 * HALF] = halves[1].astype(bf16)

    def s_near2(k):
        near(k, *line_out)

    def s_far2(k):
        start, w = chunks[k]
        mixture = far(k, *line_out)[:, 0:w]
        spread = lax.dot_general(mixture, picker, TN, preferred_element_type=f32)
        out_ref[start:start + w, :] = (
            tokens[start:start + w, :].astype(f32) + keep_ref[...] * spread
        ).astype(bf16)

    skewed([s_down, s_pair, s_sum, s_near2, s_far2])

    for copy in sends:
        copy.wait_send()
    for k in range(n_c):
        line_drain(k, zsend, z_s)
        line_drain(k, zsend2, z2_s)


def fused(tokens, passes, keep, gain, routes, gates, wg, wu, wd):
    n_z, n_e = lax.axis_size("dp"), lax.axis_size("expert")
    t_tok, width = tokens.shape
    seq_keep = routes.shape[1]
    hidden = wg.shape[2]
    turned = lambda w: jnp.swapaxes(w[0], 0, 1)
    n_c = len(chunks_of(width))
    bf16, f32 = jnp.bfloat16, jnp.float32
    vmem = pl.BlockSpec(memory_space=pltpu.VMEM)
    hbm = pl.BlockSpec(memory_space=pl.ANY)
    dma = pltpu.SemaphoreType.DMA
    rows = n_e * seq_keep
    line = pltpu.VMEM((2, n_c, seq_keep, CHUNK), bf16)
    single = pltpu.VMEM((n_c, seq_keep, CHUNK), bf16)
    block = pltpu.VMEM((n_c, n_e, HALF, CHUNK), bf16)
    both = pltpu.VMEM((n_c, 2, n_e, HALF, CHUNK), bf16)
    return pl.pallas_call(
        fused_kernel,
        out_shape=jax.ShapeDtypeStruct((width, t_tok), bf16),
        in_specs=[hbm, vmem, vmem, vmem, vmem, vmem, hbm, hbm, hbm],
        out_specs=vmem,
        scratch_shapes=[
            pltpu.VMEM((width, t_tok), bf16),
            pltpu.VMEM((hidden, width), bf16),
            pltpu.VMEM((hidden, width), bf16),
            pltpu.VMEM(wd.shape[1:], bf16),
            pltpu.VMEM((n_z, 8, t_tok), f32),
            pltpu.VMEM((2, n_e, HALF, LANES), f32),
            single, line, line,
            pltpu.VMEM((n_c, 2, HALF, CHUNK), bf16),
            both,
            pltpu.VMEM((rows, hidden), f32),
            pltpu.VMEM((rows, hidden), f32),
            pltpu.VMEM((2, rows // 2, hidden), bf16),
            both, block, block, block,
            single, line, line,
            dma((4,)), dma((n_z - 1,)), dma, dma((n_e - 1,)), dma,
            dma((2, n_c)), dma((2, n_c)),
            dma((n_c, n_e - 1)), dma((n_c,)),
            dma((n_c,)), dma((n_c,)),
            dma((n_c,)), dma((n_c,)),
            dma((n_c, n_e - 1)), dma((n_c,)),
            dma((2, n_c)), dma((2, n_c)),
        ],
        compiler_params=pltpu.CompilerParams(
            collective_id=0, has_side_effects=True, vmem_limit_bytes=58 * 1024 * 1024
        ),
    )(
        tokens.T, passes.reshape(1, t_tok), keep.reshape(1, t_tok), gain.reshape(1, width),
        turned(routes), turned(gates), turned(wg), turned(wu), wd[0],
    ).T


def rescaled_entries(rows_in, gain_row):
    scaling = lax.rsqrt(jnp.mean(rows_in * rows_in, axis=-1, keepdims=True) + 1e-05)
    return (rows_in * scaling * gain_row).astype(jnp.bfloat16)


def local(
    tokens, passes_through, keep_weight, norm_gain, routes, gate_values, w_gate, w_up, w_down
):
    piece_vectors, feature_width = tokens.shape
    batch_clusters = lax.axis_size("dp")
    experts = lax.axis_size("expert")
    most_local = 3 * (piece_vectors // 16)
    seq_keep = routes.shape[1]
    top_count = routes.shape[2]
    capacity = max(2, batch_clusters * (piece_vectors // 16) * top_count // experts * 5 // 4)
    ranking = jnp.cumsum(passes_through) - 1
    picker = (
        (ranking[None, :] == jnp.arange(most_local)[:, None]) & (passes_through[None, :] == 1)
    ).astype(jnp.bfloat16)
    compact = jnp.dot(picker, tokens, preferred_element_type=jnp.float32)
    normalized_rows = rescaled_entries(compact, norm_gain)
    remaining_total = jnp.sum(passes_through)
    gathered, counts_all = (
        lax.all_gather(normalized_rows, "dp", axis=0, tiled=True),
        lax.all_gather(remaining_total.reshape(1), "dp", axis=0, tiled=True),
    )
    offsets = jnp.cumsum(counts_all) - counts_all
    within = jnp.arange(most_local, dtype=jnp.int32)
    token_positions = (offsets[:, None] + within[None, :]).reshape(-1)
    valid_mask = (within[None, :] < counts_all[:, None]).reshape(-1)
    order_pick = (
        (token_positions[None, :] == jnp.arange(seq_keep)[:, None]) & valid_mask[None, :]
    ).astype(jnp.bfloat16)
    column_rows = jnp.dot(order_pick, gathered, preferred_element_type=jnp.float32).astype(
        jnp.bfloat16
    )
    flat_routes = routes.reshape(-1)
    onehot = (flat_routes[:, None] == jnp.arange(experts)[None, :]).astype(jnp.int32)
    slot_rank = jnp.sum((jnp.cumsum(onehot, axis=0) - onehot) * onehot, axis=1)
    targets = (flat_routes * capacity + slot_rank).reshape(seq_keep, top_count)
    slot_ids = jnp.arange(experts * capacity)
    dispatch = jnp.any(targets[None, :, :] == slot_ids[:, None, None], axis=-1).astype(jnp.bfloat16)
    buffer = jnp.dot(dispatch, column_rows, preferred_element_type=jnp.float32).astype(jnp.bfloat16)
    received = lax.all_to_all(buffer, "expert", split_axis=0, concat_axis=0, tiled=True)
    gate_proj = jnp.dot(received, w_gate[0], preferred_element_type=jnp.float32)
    up_proj = jnp.dot(received, w_up[0], preferred_element_type=jnp.float32)
    hidden = ((up_proj + 1.0) * gate_proj * jax.nn.sigmoid(1.702 * gate_proj)).astype(jnp.bfloat16)
    partials = jnp.dot(hidden, w_down[0], preferred_element_type=jnp.float32)
    summed = lax.psum_scatter(partials.astype(jnp.bfloat16), "dp", scatter_dimension=1, tiled=True)
    returned = lax.all_to_all(summed, "expert", split_axis=0, concat_axis=0, tiled=True)
    combine_weights = jnp.sum(
        (targets[:, :, None] == slot_ids[None, None, :]).astype(jnp.float32)
        * gate_values[0][:, :, None],
        axis=1,
    )
    mixture = jnp.dot(
        combine_weights, returned.astype(jnp.float32), precision=lax.Precision.HIGHEST
    )
    moe_rows = mixture.astype(jnp.bfloat16)
    owned = jnp.dot(order_pick.T, moe_rows, preferred_element_type=jnp.float32).astype(jnp.bfloat16)
    own_rows = lax.all_to_all(owned, "dp", split_axis=0, concat_axis=1, tiled=True)
    spread = jnp.dot(picker.T, own_rows, preferred_element_type=jnp.float32)
    result = tokens.astype(jnp.float32) + keep_weight[:, None] * spread
    return result.astype(jnp.bfloat16)


def layer(tokens, passes_through, keep_weight, norm_gain, routes, gate_values, w_gate, w_up, w_down):
    lines, experts = lax.axis_size("dp"), lax.axis_size("expert")
    fits = lines == 4 and experts % 2 == 0 and experts * routes.shape[1] <= 512
    step = fused if fits and routes.shape[1] == 2 * HALF and experts <= LANES else local
    return step(
        tokens, passes_through, keep_weight, norm_gain, routes, gate_values, w_gate, w_up, w_down
    )


def solution(mesh):
    return jax.shard_map(
        layer,
        mesh=mesh,
        in_specs=(
            P(("expert", "dp"), None),
            P(("expert", "dp")),
            P(("expert", "dp")),
            P(),
            P("expert", None, None),
            P("expert", None, None),
            P("expert", None, "dp"),
            P("expert", None, "dp"),
            P("expert", "dp", None),
        ),
        out_specs=P(("expert", "dp"), None),
        check_vma=False,
    )
```

```python
import jax
import jax.numpy as jnp
from jax import lax
from jax.experimental import pallas as pl
from jax.experimental.pallas import tpu as pltpu
from jax.sharding import PartitionSpec as P

CHUNK = 1664
LANES = 128
HALF = 16
NT = (((1,), (1,)), ((), ()))
TN = (((0,), (0,)), ((), ()))


def chunks_of(width):
    starts = list(range(0, width, CHUNK))
    return [(s, min(CHUNK, width - s)) for s in starts]


def fused_kernel(
    tokens_hbm, passes_ref, keep_ref, gain_ref, routes_ref, gates_ref, wg_hbm, wu_hbm, wd_hbm,
    out_ref,
    tokens, wg, wu, wd, cnt, gb, own, zin, zsend, tot, x, acc_g, acc_u, hid, ob, rb, sb, rr,
    ret, zin2, zsend2,
    ld_sem, cnt_s, cnt_r, gb_s, gb_r, z_s, z_r, a_s, a_r, b_s, b_r, d_s, d_r, e_s, e_r, z2_s, z2_r,
):
    z, me = lax.axis_index("dp"), lax.axis_index("expert")
    n_z, n_e = lax.axis_size("dp"), lax.axis_size("expert")
    width = tokens.shape[0]
    chunks = chunks_of(width)
    n_c = len(chunks)
    span = [pl.ds(0, -(-w // LANES) * LANES) for _, w in chunks]
    core = lax.rem(me, 2)
    sibling = me + 1 - 2 * core
    low = z < 2
    edge = jnp.logical_or(z == 0, z == n_z - 1)
    middle = jnp.logical_not(edge)
    inward = jnp.where(low, z + 1, z - 1)
    outward = jnp.where(z == 1, 0, n_z - 1)
    lands = jnp.where(edge, 0, 1)
    f32, bf16 = jnp.float32, jnp.bfloat16

    loads = [
        pltpu.make_async_copy(tokens_hbm, tokens, ld_sem.at[0]),
        pltpu.make_async_copy(wg_hbm, wg, ld_sem.at[1]),
        pltpu.make_async_copy(wu_hbm, wu, ld_sem.at[2]),
        pltpu.make_async_copy(wd_hbm, wd, ld_sem.at[3]),
    ]
    for load in loads:
        load.start()

    barrier = pltpu.get_barrier_semaphore()
    for r in range(1, n_z):
        pl.semaphore_signal(barrier, inc=1, device_id={"dp": lax.rem(z + r, n_z)})
    for r in range(1, n_e):
        pl.semaphore_signal(barrier, inc=1, device_id={"expert": lax.rem(me + r, n_e)})

    flags = passes_ref[...].astype(f32)
    t_tok = flags.shape[1]
    sub = lax.broadcasted_iota(jnp.int32, (t_tok, t_tok), 0)
    lane = lax.broadcasted_iota(jnp.int32, (t_tok, t_tok), 1)
    wide = jnp.broadcast_to(flags, (t_tok, t_tok))
    flag_col = jnp.sum(jnp.where(lane == sub, wide, 0.0), axis=1, keepdims=True)
    rank_row = jnp.sum(jnp.where(sub <= lane, flag_col, 0.0), axis=0, keepdims=True) - 1.0

    cnt[z] = jnp.broadcast_to(flags, cnt.shape[1:])
    top, seq_keep = routes_ref.shape
    diagonal = lax.broadcasted_iota(jnp.int32, (seq_keep, seq_keep), 0) == (
        lax.broadcasted_iota(jnp.int32, (seq_keep, seq_keep), 1)
    )

    def as_column(row):
        square = jnp.broadcast_to(row, (seq_keep, seq_keep))
        return jnp.sum(jnp.where(diagonal, square, jnp.zeros_like(square)), axis=1, keepdims=True)

    e_lane = lax.broadcasted_iota(jnp.int32, (seq_keep, LANES), 1)
    weights = jnp.zeros((seq_keep, LANES), f32)
    for k in range(top):
        weights += jnp.where(
            as_column(routes_ref[k:k + 1, :].astype(f32)) == e_lane.astype(f32),
            as_column(gates_ref[k:k + 1, :]), 0.0,
        )
    gb[:, me] = weights.reshape(2, HALF, LANES)

    pl.semaphore_wait(barrier, n_z - 1 + n_e - 1)
    sends = []

    def send(src, dst, ssem, rsem, device):
        copy = pltpu.make_async_remote_copy(
            src_ref=src, dst_ref=dst, send_sem=ssem, recv_sem=rsem, device_id=device,
            device_id_type=pl.DeviceIdType.MESH,
        )
        copy.start()
        return copy

    def arrived(ref, sem):
        pltpu.make_async_copy(ref, ref, sem).wait()

    for r in range(1, n_z):
        sends.append(send(cnt.at[z], cnt.at[z], cnt_s.at[r - 1], cnt_r, {"dp": lax.rem(z + r, n_z)}))
    for r in range(1, n_e):
        sends.append(
            send(gb.at[:, me], gb.at[:, me], gb_s.at[r - 1], gb_r, {"expert": lax.rem(me + r, n_e)})
        )

    loads[0].wait()
    arrived(cnt.at[pl.ds(0, n_z - 1)], cnt_r)
    offset = jnp.zeros((1, 1), f32)
    for other in range(n_z):
        total = jnp.sum(cnt[other, 0:1, :], axis=1, keepdims=True)
        offset += jnp.where(other < z, total, 0.0)
    s_sub = lax.broadcasted_iota(jnp.int32, (seq_keep, t_tok), 0).astype(f32)
    picker = jnp.where((rank_row + offset == s_sub) & (flags > 0.5), 1.0, 0.0).astype(bf16)
    compact = lax.dot_general(picker, tokens[...], NT, preferred_element_type=f32)
    scaling = lax.rsqrt(jnp.sum(compact * compact, axis=1, keepdims=True) * (1.0 / width) + 1e-05)
    normed = (compact * scaling * gain_ref[...]).astype(bf16)

    @pl.when(edge)
    def _():
        zin[0] = jnp.zeros_like(zin[0])
        zin2[0] = jnp.zeros_like(zin2[0])

    for k, (start, w) in enumerate(chunks):
        own[k, :, 0:w] = normed[:, start:start + w]

    def line_copy(src, dst, k, which, s_sems, r_sems, device):
        return pltpu.make_async_remote_copy(
            src_ref=src, dst_ref=dst, send_sem=s_sems.at[which, k], recv_sem=r_sems,
            device_id={"dp": device}, device_id_type=pl.DeviceIdType.MESH,
        )

    def near(k, mine, into, out, s_sems, r_sems):
        @pl.when(middle)
        def _():
            arrived(into.at[0, k, :, span[k]], r_sems.at[0, k])

        out[0, k] = (mine[k].astype(f32) + into[0, k].astype(f32)).astype(bf16)
        line_copy(
            out.at[0, k, :, span[k]], into.at[lands, k, :, span[k]], k, 0, s_sems,
            r_sems.at[lands, k], inward,
        ).start()

    def far(k, mine, into, out, s_sems, r_sems):
        arrived(into.at[1, k, :, span[k]], r_sems.at[1, k])
        part = mine[k].astype(f32) + into[1, k].astype(f32)

        @pl.when(middle)
        def _():
            out[1, k] = part.astype(bf16)
            line_copy(
                out.at[1, k, :, span[k]], into.at[1, k, :, span[k]], k, 1, s_sems,
                r_sems.at[1, k], outward,
            ).start()

        return (part + into[0, k].astype(f32)).astype(bf16)

    def line_drain(k, out, s_sems):
        arrived(out.at[0, k, :, span[k]], s_sems.at[0, k])

        @pl.when(middle)
        def _():
            arrived(out.at[1, k, :, span[k]], s_sems.at[1, k])

    line_in = (own, zin, zsend, z_s, z_r)
    line_out = (ret, zin2, zsend2, z2_s, z2_r)

    def s_near(k):
        near(k, *line_in)

    def s_far(k):
        tot[k] = far(k, *line_in).reshape(2, HALF, CHUNK)
        x[k, core, me] = tot[k, core]
        for r in range(1, n_e):
            to = lax.rem(me + r, n_e)
            side = lax.rem(to, 2)
            sends.append(send(
                tot.at[k, side, :, span[k]], x.at[k, side, me, :, span[k]],
                a_s.at[k, r - 1], a_r.at[k], {"expert": to},
            ))

    def s_swap(k):
        arrived(x.at[k, core, pl.ds(0, n_e - 1), :, span[k]], a_r.at[k])
        block = x.at[k, core, :, :, span[k]]
        sends.append(send(block, block, b_s.at[k], b_r.at[k], {"expert": sibling}))

    def s_up(k):
        start, w = chunks[k]
        arrived(x.at[k, 1 - core, :, :, span[k]], b_r.at[k])
        if k == 0:
            loads[1].wait()
            loads[2].wait()
        rows = x[k].reshape(2 * n_e * HALF, CHUNK)[:, 0:w]
        g = lax.dot_general(rows, wg[:, start:start + w], NT, preferred_element_type=f32)
        u = lax.dot_general(rows, wu[:, start:start + w], NT, preferred_element_type=f32)
        if k == 0:
            acc_g[...] = g
            acc_u[...] = u
        else:
            acc_g[...] += g
            acc_u[...] += u

    def skewed(stages):
        for t in range(n_c + len(stages) - 1):
            for i, stage in enumerate(stages):
                if 0 <= t - i < n_c:
                    stage(t - i)

    skewed([s_near, s_far, s_swap, s_up])

    arrived(gb.at[:, pl.ds(0, n_e - 1)], gb_r)
    g_lane = lax.broadcasted_iota(jnp.int32, gb.shape, 3)
    gw = jnp.sum(jnp.where(g_lane == me, gb[...], 0.0), axis=3, keepdims=True)
    gw = gw.reshape(2 * n_e * HALF, 1)
    gate = acc_g[...]
    hid[...] = ((acc_u[...] + 1.0) * gate * jax.nn.sigmoid(1.702 * gate) * gw).astype(bf16).reshape(hid.shape)
    loads[3].wait()

    def down_half(k, half):
        start, w = chunks[k]
        part = jnp.dot(hid[half], wd[:, start:start + w], preferred_element_type=f32)
        ob[k, half, :, :, 0:w] = part.astype(bf16).reshape(n_e, HALF, w)

    def s_down(k):
        down_half(k, 1 - core)
        sends.append(send(
            ob.at[k, 1 - core, :, :, span[k]], rb.at[k, :, :, span[k]],
            d_s.at[k], d_r.at[k], {"expert": sibling},
        ))

    def s_pair(k):
        down_half(k, core)
        arrived(rb.at[k, :, :, span[k]], d_r.at[k])
        sb[k] = (ob[k, core].astype(f32) + rb[k].astype(f32)).astype(bf16)
        rr[k, me] = sb[k, me]
        for r in range(1, n_e):
            to = lax.rem(me + r, n_e)
            sends.append(send(
                sb.at[k, to, :, span[k]], rr.at[k, me, :, span[k]],
                e_s.at[k, r - 1], e_r.at[k], {"expert": to},
            ))

    def s_sum(k):
        arrived(rr.at[k, pl.ds(0, n_e - 1), :, span[k]], e_r.at[k])
        halves = [
            sum(rr[k, 2 * j + h].astype(f32) for j in range(n_e // 2)) for h in range(2)
        ]
        ret[k, 0:HALF] = halves[0].astype(bf16)
        ret[k, HALF:2 * HALF] = halves[1].astype(bf16)

    def s_near2(k):
        near(k, *line_out)

    def s_far2(k):
        start, w = chunks[k]
        mixture = far(k, *line_out)[:, 0:w]
        spread = lax.dot_general(mixture, picker, TN, preferred_element_type=f32)
        out_ref[start:start + w, :] = (
            tokens[start:start + w, :].astype(f32) + keep_ref[...] * spread
        ).astype(bf16)

    skewed([s_down, s_pair, s_sum, s_near2, s_far2])

    for copy in sends:
        copy.wait_send()
    for k in range(n_c):
        line_drain(k, zsend, z_s)
        line_drain(k, zsend2, z2_s)


def fused(tokens, passes, keep, gain, routes, gates, wg, wu, wd):
    n_z, n_e = lax.axis_size("dp"), lax.axis_size("expert")
    t_tok, width = tokens.shape
    seq_keep = routes.shape[1]
    hidden = wg.shape[2]
    turned = lambda w: jnp.swapaxes(w[0], 0, 1)
    n_c = len(chunks_of(width))
    bf16, f32 = jnp.bfloat16, jnp.float32
    vmem = pl.BlockSpec(memory_space=pltpu.VMEM)
    hbm = pl.BlockSpec(memory_space=pl.ANY)
    dma = pltpu.SemaphoreType.DMA
    rows = n_e * seq_keep
    line = pltpu.VMEM((2, n_c, seq_keep, CHUNK), bf16)
    single = pltpu.VMEM((n_c, seq_keep, CHUNK), bf16)
    block = pltpu.VMEM((n_c, n_e, HALF, CHUNK), bf16)
    both = pltpu.VMEM((n_c, 2, n_e, HALF, CHUNK), bf16)
    return pl.pallas_call(
        fused_kernel,
        out_shape=jax.ShapeDtypeStruct((width, t_tok), bf16),
        in_specs=[hbm, vmem, vmem, vmem, vmem, vmem, hbm, hbm, hbm],
        out_specs=vmem,
        scratch_shapes=[
            pltpu.VMEM((width, t_tok), bf16),
            pltpu.VMEM((hidden, width), bf16),
            pltpu.VMEM((hidden, width), bf16),
            pltpu.VMEM(wd.shape[1:], bf16),
            pltpu.VMEM((n_z, 8, t_tok), f32),
            pltpu.VMEM((2, n_e, HALF, LANES), f32),
            single, line, line,
            pltpu.VMEM((n_c, 2, HALF, CHUNK), bf16),
            both,
            pltpu.VMEM((rows, hidden), f32),
            pltpu.VMEM((rows, hidden), f32),
            pltpu.VMEM((2, rows // 2, hidden), bf16),
            both, block, block, block,
            single, line, line,
            dma((4,)), dma((n_z - 1,)), dma, dma((n_e - 1,)), dma,
            dma((2, n_c)), dma((2, n_c)),
            dma((n_c, n_e - 1)), dma((n_c,)),
            dma((n_c,)), dma((n_c,)),
            dma((n_c,)), dma((n_c,)),
            dma((n_c, n_e - 1)), dma((n_c,)),
            dma((2, n_c)), dma((2, n_c)),
        ],
        compiler_params=pltpu.CompilerParams(
            collective_id=0, has_side_effects=True, vmem_limit_bytes=58 * 1024 * 1024
        ),
    )(
        tokens.T, passes.reshape(1, t_tok), keep.reshape(1, t_tok), gain.reshape(1, width),
        turned(routes), turned(gates), turned(wg), turned(wu), wd[0],
    ).T


def rescaled_entries(rows_in, gain_row):
    scaling = lax.rsqrt(jnp.mean(rows_in * rows_in, axis=-1, keepdims=True) + 1e-05)
    return (rows_in * scaling * gain_row).astype(jnp.bfloat16)


def local(
    tokens, passes_through, keep_weight, norm_gain, routes, gate_values, w_gate, w_up, w_down
):
    piece_vectors, feature_width = tokens.shape
    batch_clusters = lax.axis_size("dp")
    experts = lax.axis_size("expert")
    most_local = 3 * (piece_vectors // 16)
    seq_keep = routes.shape[1]
    top_count = routes.shape[2]
    capacity = max(2, batch_clusters * (piece_vectors // 16) * top_count // experts * 5 // 4)
    ranking = jnp.cumsum(passes_through) - 1
    picker = (
        (ranking[None, :] == jnp.arange(most_local)[:, None]) & (passes_through[None, :] == 1)
    ).astype(jnp.bfloat16)
    compact = jnp.dot(picker, tokens, preferred_element_type=jnp.float32)
    normalized_rows = rescaled_entries(compact, norm_gain)
    remaining_total = jnp.sum(passes_through)
    gathered, counts_all = (
        lax.all_gather(normalized_rows, "dp", axis=0, tiled=True),
        lax.all_gather(remaining_total.reshape(1), "dp", axis=0, tiled=True),
    )
    offsets = jnp.cumsum(counts_all) - counts_all
    within = jnp.arange(most_local, dtype=jnp.int32)
    token_positions = (offsets[:, None] + within[None, :]).reshape(-1)
    valid_mask = (within[None, :] < counts_all[:, None]).reshape(-1)
    order_pick = (
        (token_positions[None, :] == jnp.arange(seq_keep)[:, None]) & valid_mask[None, :]
    ).astype(jnp.bfloat16)
    column_rows = jnp.dot(order_pick, gathered, preferred_element_type=jnp.float32).astype(
        jnp.bfloat16
    )
    flat_routes = routes.reshape(-1)
    onehot = (flat_routes[:, None] == jnp.arange(experts)[None, :]).astype(jnp.int32)
    slot_rank = jnp.sum((jnp.cumsum(onehot, axis=0) - onehot) * onehot, axis=1)
    targets = (flat_routes * capacity + slot_rank).reshape(seq_keep, top_count)
    slot_ids = jnp.arange(experts * capacity)
    dispatch = jnp.any(targets[None, :, :] == slot_ids[:, None, None], axis=-1).astype(jnp.bfloat16)
    buffer = jnp.dot(dispatch, column_rows, preferred_element_type=jnp.float32).astype(jnp.bfloat16)
    received = lax.all_to_all(buffer, "expert", split_axis=0, concat_axis=0, tiled=True)
    gate_proj = jnp.dot(received, w_gate[0], preferred_element_type=jnp.float32)
    up_proj = jnp.dot(received, w_up[0], preferred_element_type=jnp.float32)
    hidden = ((up_proj + 1.0) * gate_proj * jax.nn.sigmoid(1.702 * gate_proj)).astype(jnp.bfloat16)
    partials = jnp.dot(hidden, w_down[0], preferred_element_type=jnp.float32)
    summed = lax.psum_scatter(partials.astype(jnp.bfloat16), "dp", scatter_dimension=1, tiled=True)
    returned = lax.all_to_all(summed, "expert", split_axis=0, concat_axis=0, tiled=True)
    combine_weights = jnp.sum(
        (targets[:, :, None] == slot_ids[None, None, :]).astype(jnp.float32)
        * gate_values[0][:, :, None],
        axis=1,
    )
    mixture = jnp.dot(
        combine_weights, returned.astype(jnp.float32), precision=lax.Precision.HIGHEST
    )
    moe_rows = mixture.astype(jnp.bfloat16)
    owned = jnp.dot(order_pick.T, moe_rows, preferred_element_type=jnp.float32).astype(jnp.bfloat16)
    own_rows = lax.all_to_all(owned, "dp", split_axis=0, concat_axis=1, tiled=True)
    spread = jnp.dot(picker.T, own_rows, preferred_element_type=jnp.float32)
    result = tokens.astype(jnp.float32) + keep_weight[:, None] * spread
    return result.astype(jnp.bfloat16)


def layer(tokens, passes_through, keep_weight, norm_gain, routes, gate_values, w_gate, w_up, w_down):
    lines, experts = lax.axis_size("dp"), lax.axis_size("expert")
    fits = lines == 4 and experts % 2 == 0 and experts * routes.shape[1] <= 512
    step = fused if fits and routes.shape[1] == 2 * HALF and experts <= LANES else local
    return step(
        tokens, passes_through, keep_weight, norm_gain, routes, gate_values, w_gate, w_up, w_down
    )


def solution(mesh):
    return jax.shard_map(
        layer,
        mesh=mesh,
        in_specs=(
            P(("expert", "dp"), None),
            P(("expert", "dp")),
            P(("expert", "dp")),
            P(),
            P("expert", None, None),
            P("expert", None, None),
            P("expert", None, "dp"),
            P("expert", None, "dp"),
            P("expert", "dp", None),
        ),
        out_specs=P(("expert", "dp"), None),
        check_vma=False,
    )
```
